128 devices in a mesh: row: 8 (over x, z_lo), col: 16 (over z_hi, y, core).
Axes of the slice: x: 4, y: 4, z: 4 (z_hi: 2, z_lo: 2; z = z_hi * 2 + z_lo), core: 2. Of those that a mesh axis runs over, the one named last changes fastest.
Arguments:
- thermal_field_values: float32 [256, 1024, 1024], P('col', 'row'), may hold values from -6 to 6
- particle_entry_location: int32 [3, 8388608], P(None, ('row', 'col')), may hold values from 0 to 1023, as said below
- particle_condensation_energy: float32 [8388608], P(('row', 'col')), may hold values from -96 to 96
- tube_particle_tally: int32 [128], P(('row', 'col')), may hold values from 16384 to 65536, as said below
- eigen_decay_factors: float32 [256], replicated, may hold values from 0.05 to 2
- stratum_eigen_analysis: bfloat16 [256, 256], replicated, may hold values from -0.375 to 0.375
- eigen_synthesis_matrix: bfloat16 [256, 256], replicated, may hold values from -0.375 to 0.375
Outputs:
- updated: float32 [256, 1024, 1024], P('col', 'row')
The draws below stay inside these ranges and needn't reach their ends.
Inputs may be any that keep to these rules, and one draw needn't show every extreme that they name: particle_entry_location[0] lies below 1024, particle_entry_location[1] below 128, particle_entry_location[2] below 16, for every slot, padding slots too. `tube_particle_tally`: at least one pencil is full.
All inputs are finite; a program needn't handle non-finite values.
Results may differ from the reference program's by a relative error of at most 0.011.
Values may be sent and summed in bfloat16 or wider, within the bound.
A program may use at most 128 MiB of HBM per device.

```python
import math
import jax
import jax.numpy as jnp

SAMPLES_EAST = 1024
SAMPLES_NORTH = 1024
STRATA_NUMBER = 256
DROP_DEV = 65536
CY = 128
CZ = 16
DROPS = 8388608
N_ROW = 8
N_COL = 16


def draw_particle_entry_location(key, part):
    key = jax.random.fold_in(key, 11)
    first, second, third = jax.random.split(key, 3)
    along_x = jax.random.randint(first, (DROPS,), 0, SAMPLES_EAST, dtype=jnp.int32)
    along_y = jax.random.randint(second, (DROPS,), 0, CY, dtype=jnp.int32)
    along_z = jax.random.randint(third, (DROPS,), 0, CZ, dtype=jnp.int32)
    return jnp.stack([along_x, along_y, along_z], axis=0)


def draw_tube_particle_tally(key, part):
    key = jax.random.fold_in(key, 23)
    first, second = jax.random.split(key, 2)
    pencils = N_ROW * N_COL
    base = jax.random.randint(first, (pencils,), DROP_DEV // 4, DROP_DEV + 1, dtype=jnp.int32)
    fullest = jax.random.randint(second, (), 0, pencils, dtype=jnp.int32)
    return jnp.where(jnp.arange(pencils, dtype=jnp.int32) == fullest, DROP_DEV, base).astype(jnp.int32)


def block_levels(stream_key, dims, cuts, low, high):
    gain, own = 1.0, jax.random.fold_in(stream_key, 6)
    for position, blocks in cuts:
        steps = jnp.exp(jax.random.uniform(jax.random.fold_in(own, position), (blocks,), jnp.float32, low / len(cuts), high / len(cuts)))
        gain = gain * jnp.repeat(steps, dims[position] // blocks).reshape([-1 if axis == position else 1 for axis in range(len(dims))])
    return gain


def noise(own_key, extent, deviation, bound, pieces=(), held_as=jnp.bfloat16):
    level = block_levels(own_key, extent, pieces, -0.22, 0.18) if pieces else 1.0
    entries = jax.random.normal(own_key, extent, jnp.float32) * deviation * level
    return jnp.minimum(jnp.maximum(entries, -bound), bound).astype(held_as)


def setup_inputs(seed: int = 0) -> dict:
    streams_of = jax.random.split(jax.random.key(seed), 8)
    thermal_field_values = noise(streams_of[0], (STRATA_NUMBER, SAMPLES_NORTH, SAMPLES_EAST), 1.0, 6.0, ((0, 16), (1, 8)), jnp.float32)
    particle_entry_location = draw_particle_entry_location(jax.random.fold_in(streams_of[7], 71), 0)
    particle_condensation_energy = noise(streams_of[2], (DROPS,), 16.0, 96.0, ((0, 128),), jnp.float32)
    tube_particle_tally = draw_tube_particle_tally(jax.random.fold_in(streams_of[7], 71), 0)
    eigen_decay_factors = jnp.clip(jnp.exp(jax.random.uniform(streams_of[4], (STRATA_NUMBER,), jnp.float32, math.log(0.05), math.log(2.0))), 0.05, 2.0)
    stratum_eigen_analysis = noise(streams_of[5], (STRATA_NUMBER, STRATA_NUMBER), STRATA_NUMBER ** -0.5, 0.375)
    eigen_synthesis_matrix = noise(streams_of[6], (STRATA_NUMBER, STRATA_NUMBER), STRATA_NUMBER ** -0.5, 0.375)
    return {"thermal_field_values": thermal_field_values, "particle_entry_location": particle_entry_location, "particle_condensation_energy": particle_condensation_energy, "tube_particle_tally": tube_particle_tally, "eigen_decay_factors": eigen_decay_factors, "stratum_eigen_analysis": stratum_eigen_analysis, "eigen_synthesis_matrix": eigen_synthesis_matrix}


DIFFUSION = 0.1

def cas_table(row_index, col_index, length):
    product = row_index[:, None] * col_index[None, :] % length
    angle = product.astype(jnp.float32) * (2.0 * math.pi / length)
    return ((jnp.cos(angle) + jnp.sin(angle)) * (1.0 / math.sqrt(length))).astype(jnp.bfloat16)

def wave_square(index, length):
    folded = jnp.minimum(index, length - index).astype(jnp.float32)
    return (folded * (2.0 * math.pi / length)) ** 2

def reference(thermal_field_values, particle_entry_location, particle_condensation_energy, tube_particle_tally, eigen_decay_factors, stratum_eigen_analysis, eigen_synthesis_matrix):
    order = jnp.arange(DROPS, dtype=jnp.int32)
    block = order // DROP_DEV
    live = order % DROP_DEV < tube_particle_tally[block]
    zglobal = block % N_COL * CZ + particle_entry_location[2]
    yglobal = block // N_COL * CY + particle_entry_location[1]
    flat = (zglobal * SAMPLES_NORTH + yglobal) * SAMPLES_EAST + particle_entry_location[0]
    deposit = jax.ops.segment_sum(jnp.where(live, particle_condensation_energy, jnp.float32(0.0)), flat, num_segments=STRATA_NUMBER * SAMPLES_NORTH * SAMPLES_EAST).reshape(STRATA_NUMBER, SAMPLES_NORTH, SAMPLES_EAST)
    padded = jnp.pad(deposit, ((1, 1), (0, 0), (0, 0)))
    along_z = 0.25 * (padded[:-2] + padded[2:]) + 0.5 * padded[1:-1]
    along_y = 0.25 * (jnp.roll(along_z, 1, 1) + jnp.roll(along_z, -1, 1)) + 0.5 * along_z
    condensation_warming = 0.25 * (jnp.roll(along_y, 1, 2) + jnp.roll(along_y, -1, 2)) + 0.5 * along_y
    thermal_source_term = (thermal_field_values + condensation_warming).astype(jnp.bfloat16)
    index_x = jnp.arange(SAMPLES_EAST, dtype=jnp.int32)
    index_y = jnp.arange(SAMPLES_NORTH, dtype=jnp.int32)
    table_x = cas_table(index_x, index_x, SAMPLES_EAST).astype(jnp.float32)
    table_y = cas_table(index_y, index_y, SAMPLES_NORTH).astype(jnp.float32)
    along_x = jnp.dot(thermal_source_term.astype(jnp.float32), table_x).astype(jnp.bfloat16)
    spectrum = jnp.einsum('zyx,ym->zmx', along_x.astype(jnp.float32), table_y).astype(jnp.bfloat16)
    modal = jnp.einsum('wz,zmx->wmx', stratum_eigen_analysis.astype(jnp.float32), spectrum.astype(jnp.float32))
    denom = 1.0 + DIFFUSION * (wave_square(index_y, SAMPLES_NORTH)[None, :, None] + wave_square(index_x, SAMPLES_EAST)[None, None, :]) + eigen_decay_factors[:, None, None]
    scaled = (modal / denom).astype(jnp.bfloat16)
    levels = jnp.einsum('zw,wmx->zmx', eigen_synthesis_matrix.astype(jnp.float32), scaled.astype(jnp.float32)).astype(jnp.bfloat16)
    back_y = jnp.einsum('zmx,my->zyx', levels.astype(jnp.float32), table_y).astype(jnp.bfloat16)
    return jnp.dot(back_y.astype(jnp.float32), table_x)
```

```python
import functools
import math

import jax
import jax.numpy as jnp
import ml_dtypes
import numpy as np
from jax import lax
from jax.experimental import pallas as pl
from jax.experimental.pallas import tpu as pltpu
from jax.sharding import PartitionSpec as P

DIFFUSION = 0.1
MESH = pl.DeviceIdType.MESH
F32 = jnp.float32
BF16 = jnp.bfloat16
ROWS, COLS = 8, 16
DEVICES = ROWS * COLS
NX = NY = 1024
NZ = 256
CY, CZ = 128, 16
OWN = NX // DEVICES
PARTS = 4
QUAD = CZ // PARTS
MSG = QUAD * OWN
PHASES = 4
PAIR = OWN // PHASES
ORDER = (1, 2, 0, 3)
LANES = 128


def cas_table(length):
    index = np.arange(length)
    angle = (index[:, None] * index[None, :] % length) * (2.0 * math.pi / length)
    return ((np.cos(angle) + np.sin(angle)) / math.sqrt(length)).astype(ml_dtypes.bfloat16)


def dot(a, b, contract):
    return lax.dot_general(a, b, (contract, ((), ())), preferred_element_type=F32)


def partner(row, col, i):
    j = lax.rem(i * 37, DEVICES)
    x, z_lo = row // 2, lax.rem(row, 2)
    z_hi, y, core = col // 8, lax.rem(col // 2, 4), lax.rem(col, 2)
    x = lax.rem(x + j // 32, 4)
    y = lax.rem(y + lax.rem(j // 8, 4), 4)
    z = lax.rem(z_hi * 2 + z_lo + lax.rem(j // 2, 4), 4)
    core = lax.rem(core + lax.rem(j, 2), 2)
    return x * 2 + lax.rem(z, 2), (z // 2) * 8 + y * 2 + core


def spectral_kernel(
    deposit, thermal, table, analysis, synthesis, damping, wave_y,
    home,
    padded, field, forcing, outgoing, incoming, lines, solved, modes,
    edge_lo, edge_hi, halo_lo, halo_hi, corners, plane_out, plane_in,
    load_sems, edge_send, edge_recv, send_sems, recv_sems, own_sems, back_send, back_recv, back_own,
):
    row, col = lax.axis_index("row"), lax.axis_index("col")
    me = row * COLS + col
    barrier = pltpu.get_barrier_semaphore()

    def greet(i, carry):
        r, c = partner(row, col, i)
        pl.semaphore_signal(barrier, inc=1, device_id=(r, c), device_id_type=MESH)
        return carry

    deposit_load = pltpu.make_async_copy(
        deposit, padded.at[pl.ds(1, CZ), pl.ds(8, CY), :], load_sems.at[0]
    )
    deposit_load.start()
    field_load = pltpu.make_async_copy(thermal, field, load_sems.at[1])
    field_load.start()
    lax.fori_loop(1, DEVICES, greet, 0)
    deposit_load.wait()

    for z in range(CZ):
        edge_lo[z : z + 1, :] = padded[1 + z, 8:9, :]
        edge_hi[z : z + 1, :] = padded[1 + z, 7 + CY : 8 + CY, :]
    plane_out[0] = padded[1, 8 : 8 + CY, :].astype(BF16)
    plane_out[1] = padded[CZ, 8 : 8 + CY, :].astype(BF16)
    pl.semaphore_wait(barrier, DEVICES - 1)
    row_up, row_dn = lax.rem(row + 1, ROWS), lax.rem(row + ROWS - 1, ROWS)
    col_up, col_dn = lax.rem(col + 1, COLS), lax.rem(col + COLS - 1, COLS)
    top, low = pl.ds(CZ - 8, 8), pl.ds(0, 8)
    halo_copies = []
    for n, (src, dst, where) in enumerate((
        (edge_hi, halo_lo, (row_up, col)),
        (edge_lo, halo_hi, (row_dn, col)),
        (edge_hi.at[top], corners.at[0], (row_up, col_up)),
        (edge_lo.at[top], corners.at[1], (row_dn, col_up)),
        (edge_hi.at[low], corners.at[2], (row_up, col_dn)),
        (edge_lo.at[low], corners.at[3], (row_dn, col_dn)),
        (plane_out.at[1], plane_in.at[0], (row, col_up)),
        (plane_out.at[0], plane_in.at[1], (row, col_dn)),
    )):
        copy = pltpu.make_async_remote_copy(
            src, dst, edge_send.at[n], edge_recv.at[n], device_id=where, device_id_type=MESH
        )
        copy.start()
        halo_copies.append(copy)
    for n in (0, 1):
        halo_copies[n].wait_recv()
    for z in range(CZ):
        padded[1 + z, 7:8, :] = halo_lo[z : z + 1, :]
        padded[1 + z, 8 + CY : 9 + CY, :] = halo_hi[z : z + 1, :]
    field_load.wait()

    def smooth(part):
        def block(n, carry):
            level = part * QUAD + n // 4
            start = pl.multiple_of(lax.rem(n, 4) * 32, 32)
            window = pl.ds(start, 48)
            mixed = 0.5 * padded[level + 1, window, :] + 0.25 * (
                padded[level, window, :] + padded[level + 2, window, :]
            )
            mixed = 0.5 * mixed[8:40] + 0.25 * (mixed[7:39] + mixed[9:41])
            mixed = 0.5 * mixed + 0.25 * (pltpu.roll(mixed, 1, 1) + pltpu.roll(mixed, NX - 1, 1))
            total = field[level, pl.ds(start, 32), :] + mixed
            forcing[pl.ds(pl.multiple_of(n * 32, 32), 32), :] = total.astype(BF16)
            return carry

        lax.fori_loop(0, 4 * QUAD, block, 0)

    def along_x(part):
        def block(n, carry):
            k = pl.multiple_of(n * 256, 256)
            out = dot(table[pl.ds(k, 256), :], forcing[...], ((1,), (1,)))
            for pair in range(QUAD // 2):
                both = [
                    out[:, z * CY : (z + 1) * CY].reshape(32, OWN, CY)
                    for z in (2 * pair, 2 * pair + 1)
                ]
                outgoing[part, pl.ds(n * 32, 32), pair * 16 : pair * 16 + 16, :] = jnp.concatenate(
                    both, axis=1
                ).astype(BF16)
            return carry

        lax.fori_loop(0, NX // 256, block, 0)

    def landing(part):
        return incoming.at[
            part,
            pl.ds(pl.multiple_of(col * MSG, MSG), MSG),
            pl.ds(pl.multiple_of(row * CY, CY), CY),
        ]

    def send(part):
        def one(i, carry):
            r, c = partner(row, col, i)
            pltpu.make_async_remote_copy(
                outgoing.at[part, r * COLS + c], landing(part), send_sems.at[part], recv_sems.at[part],
                device_id=(r, c), device_id_type=MESH,
            ).start()
            return carry

        lax.fori_loop(1, DEVICES, one, 0)
        own = pltpu.make_async_copy(outgoing.at[part, me], landing(part), own_sems.at[part])
        own.start()
        return own

    owns = {}
    for part in ORDER:
        if part == ORDER[2]:
            for copy in halo_copies[2:]:
                copy.wait_recv()
            below, above = plane_in[0].astype(F32), plane_in[1].astype(F32)
            has_below, has_above = col > 0, col < COLS - 1
            padded[0, 8 : 8 + CY, :] = jnp.where(has_below, below, 0.0)
            padded[CZ + 1, 8 : 8 + CY, :] = jnp.where(has_above, above, 0.0)
            padded[0, 7:8, :] = jnp.where(has_below, corners[0, 7:8, :], 0.0)
            padded[0, 8 + CY : 9 + CY, :] = jnp.where(has_below, corners[1, 7:8, :], 0.0)
            padded[CZ + 1, 7:8, :] = jnp.where(has_above, corners[2, 0:1, :], 0.0)
            padded[CZ + 1, 8 + CY : 9 + CY, :] = jnp.where(has_above, corners[3, 0:1, :], 0.0)
        smooth(part)
        along_x(part)
        owns[part] = send(part)

    for part in ORDER:
        owns[part].wait()
        arrived = outgoing.at[part, pl.ds(0, DEVICES - 1)]
        pltpu.make_async_copy(arrived, arrived, recv_sems.at[part]).wait()

        def along_y(n, carry, part=part):
            rows = pl.ds(pl.multiple_of(n * 128, 128), 128)
            out = dot(incoming[part, rows, :], table[...], ((1,), (0,)))
            for tile in range(NY // LANES):
                lines[part, tile, rows, :] = out[:, tile * LANES : (tile + 1) * LANES]
            return carry

        lax.fori_loop(0, COLS * MSG // 128, along_y, 0)

    def solve(k, carry):
        wave = me * OWN + k
        folded = jnp.minimum(wave, NX - wave).astype(F32) * (2.0 * math.pi / NX)
        base = 1.0 + DIFFUSION * folded * folded

        def strip(n, c):
            m = pl.ds(pl.multiple_of(n * 256, 256), 256)
            every = pl.ds(k, COLS * QUAD, stride=OWN)
            planes = jnp.concatenate(
                [
                    jnp.concatenate([lines[part, 2 * n + t, every, :] for t in range(2)], axis=1)
                    for part in range(PARTS)
                ],
                axis=0,
            ).astype(BF16)
            modal = dot(analysis[...], planes, ((1,), (0,)))
            denom = (base + DIFFUSION * wave_y[0:1, m]) + damping[...]
            scaled = (modal / denom).astype(BF16)
            modes[:, m] = dot(synthesis[...], scaled, ((1,), (0,))).astype(BF16)
            return c

        lax.fori_loop(0, NY // 256, strip, 0)

        def back(n, c):
            rows = pl.ds(pl.multiple_of(n * 128, 128), 128)
            solved[k, rows, :] = dot(modes[rows, :], table[...], ((1,), (0,))).astype(BF16)
            return c

        lax.fori_loop(0, NZ // 128, back, 0)
        return carry

    def piece(phase, r, c):
        return solved.at[
            pl.ds(phase * PAIR, PAIR),
            pl.ds(pl.multiple_of(c * CZ, CZ), CZ),
            pl.ds(pl.multiple_of(r * CY, CY), CY),
        ]

    back_owns = []
    for phase in range(PHASES):
        lax.fori_loop(phase * PAIR, (phase + 1) * PAIR, solve, 0)
        place = home.at[pl.ds(me * OWN + phase * PAIR, PAIR)]

        def give(i, carry, phase=phase, place=place):
            r, c = partner(row, col, i)
            pltpu.make_async_remote_copy(
                piece(phase, r, c), place, back_send, back_recv, device_id=(r, c), device_id_type=MESH
            ).start()
            return carry

        lax.fori_loop(1, DEVICES, give, 0)
        own = pltpu.make_async_copy(piece(phase, row, col), place, back_own.at[phase])
        own.start()
        back_owns.append(own)

    for own in back_owns:
        own.wait()
    everything = home.at[pl.ds(0, NX - OWN)]
    pltpu.make_async_copy(everything, everything, back_recv).wait()
    pltpu.make_async_copy(everything, everything, back_send).wait()
    for part in range(PARTS):
        sent = outgoing.at[part, pl.ds(0, DEVICES - 1)]
        pltpu.make_async_copy(sent, sent, send_sems.at[part]).wait()
    for copy in halo_copies:
        copy.wait_send()


def spectral_step(deposit, thermal, table, analysis, synthesis, damping, wave_y):
    any_space, vmem = pl.BlockSpec(memory_space=pl.ANY), pl.BlockSpec(memory_space=pltpu.VMEM)
    return pl.pallas_call(
        spectral_kernel,
        out_shape=jax.ShapeDtypeStruct((NX, CZ, CY), BF16),
        in_specs=[any_space, any_space, vmem, vmem, vmem, vmem, vmem],
        out_specs=any_space,
        scratch_shapes=[
            pltpu.VMEM((CZ + 2, CY + 16, NX), F32),
            pltpu.VMEM((CZ, CY, NX), F32),
            pltpu.VMEM((QUAD * CY, NX), BF16),
            pltpu.VMEM((PARTS, DEVICES, MSG, CY), BF16),
            pltpu.VMEM((PARTS, COLS * MSG, NY), BF16),
            pltpu.VMEM((PARTS, NY // LANES, COLS * MSG, LANES), F32),
            pltpu.VMEM((OWN, NZ, NY), BF16),
            pltpu.VMEM((NZ, NY), BF16),
            pltpu.VMEM((CZ, NX), F32),
            pltpu.VMEM((CZ, NX), F32),
            pltpu.VMEM((CZ, NX), F32),
            pltpu.VMEM((CZ, NX), F32),
            pltpu.VMEM((4, 8, NX), F32),
            pltpu.VMEM((2, CY, NX), BF16),
            pltpu.VMEM((2, CY, NX), BF16),
            pltpu.SemaphoreType.DMA((2,)),
            pltpu.SemaphoreType.DMA((8,)),
            pltpu.SemaphoreType.DMA((8,)),
            pltpu.SemaphoreType.DMA((PARTS,)),
            pltpu.SemaphoreType.DMA((PARTS,)),
            pltpu.SemaphoreType.DMA((PARTS,)),
            pltpu.SemaphoreType.DMA,
            pltpu.SemaphoreType.DMA,
            pltpu.SemaphoreType.DMA((PHASES,)),
        ],
        compiler_params=pltpu.CompilerParams(
            collective_id=0, has_side_effects=True, vmem_limit_bytes=60 * 2**20
        ),
        name="spectral_step",
    )(deposit, thermal, table, analysis, synthesis, damping, wave_y)


def home_kernel(home, table, out, rows):
    @pl.when(pl.program_id(0) == 0)
    def _():
        def widen(n, carry):
            k = pl.multiple_of(n * 32, 32)
            rows[pl.ds(pl.multiple_of(n * 32 * CZ, 512), 32 * CZ), :] = (
                home[pl.ds(k, 32)].astype(F32).reshape(32 * CZ, CY)
            )
            return carry

        lax.fori_loop(0, NX // 32, widen, 0)

    level = pl.program_id(0) * 2
    both = jnp.concatenate(
        [rows[pl.ds(level + z, NX, stride=CZ), :].astype(BF16) for z in range(2)], axis=1
    )
    for x in range(0, NX, 256):
        part = dot(both, table[:, x : x + 256], ((0,), (0,)))
        out[:, :, x : x + 256] = part.reshape(2, CY, 256)


def home_step(home, table):
    return pl.pallas_call(
        home_kernel,
        grid=(CZ // 2,),
        out_shape=jax.ShapeDtypeStruct((CZ, CY, NX), F32),
        in_specs=[
            pl.BlockSpec((NX, CZ, CY), lambda i: (0, 0, 0)),
            pl.BlockSpec((NX, NX), lambda i: (0, 0)),
        ],
        out_specs=pl.BlockSpec((2, CY, NX), lambda i: (i, 0, 0)),
        scratch_shapes=[pltpu.VMEM((NX * CZ, CY), F32)],
        compiler_params=pltpu.CompilerParams(vmem_limit_bytes=50 * 2**20),
        name="home_step",
    )(home, table)


def scatter(location, energy, tally):
    live = jnp.arange(energy.shape[0], dtype=jnp.int32) < tally[0]
    flat = (location[2] * CY + location[1]) * NX + location[0]
    return jax.ops.segment_sum(
        jnp.where(live, energy, 0.0), flat, num_segments=CZ * CY * NX
    ).reshape(CZ, CY, NX)


def body(thermal, location, energy, tally, decay, analysis, synthesis):
    deposit = scatter(location, energy, tally)
    table = jnp.asarray(cas_table(NX))
    analysis = analysis.reshape(NZ, COLS, PARTS, QUAD).transpose(0, 2, 1, 3).reshape(NZ, NZ)
    index = np.arange(NY)
    wave_y = ((np.minimum(index, NY - index) * (2.0 * math.pi / NY)) ** 2).astype(np.float32)
    home = spectral_step(
        deposit, thermal, table, analysis, synthesis, decay[:, None], jnp.asarray(wave_y)[None, :]
    )
    return home_step(home, table)


def solution(mesh):
    in_specs = (
        P("col", "row", None),
        P(None, ("row", "col")),
        P(("row", "col")),
        P(("row", "col")),
        P(),
        P(),
        P(),
    )
    return jax.shard_map(
        body, mesh=mesh, in_specs=in_specs, out_specs=P("col", "row", None), check_vma=False
    )
```

```python
import functools
import math

import jax
import jax.numpy as jnp
import ml_dtypes
import numpy as np
from jax import lax
from jax.experimental import pallas as pl
from jax.experimental.pallas import tpu as pltpu
from jax.sharding import PartitionSpec as P

DIFFUSION = 0.1
MESH = pl.DeviceIdType.MESH
F32 = jnp.float32
BF16 = jnp.bfloat16
ROWS, COLS = 8, 16
DEVICES = ROWS * COLS
NX = NY = 1024
NZ = 256
CY, CZ = 128, 16
OWN = NX // DEVICES
PARTS = 4
QUAD = CZ // PARTS
MSG = QUAD * OWN
PHASES = (0, 1, 3, 5, 7, 8)
ORDER = (1, 2, 0, 3)
LANES = 128
WINDOW = 6
GROUPS = CZ * NX // LANES


def cas_table(length):
    index = np.arange(length)
    angle = (index[:, None] * index[None, :] % length) * (2.0 * math.pi / length)
    return ((np.cos(angle) + np.sin(angle)) / math.sqrt(length)).astype(ml_dtypes.bfloat16)


def dot(a, b, contract):
    return lax.dot_general(a, b, (contract, ((), ())), preferred_element_type=F32)


def for_partners(row, col, act):
    x, y, z, core = row >> 1, (col >> 1) & 3, ((col >> 3) << 1) + (row & 1), col & 1
    depths = [(z + t) & 3 for t in range(4)]
    z_row = [depth & 1 for depth in depths]
    z_col = [((depth >> 1) << 3) + c for depth in depths for c in (core, core ^ 1)]

    def group(x, y, skip):
        for t in range(4):
            r = (((x + t) & 3) << 1) + z_row[t]
            near = ((y + t) & 3) << 1
            for c in range(2):
                if t or c or not skip:
                    act(r, z_col[2 * t + c] + near)

    def step(i, carry):
        group(x + (i >> 2), y + (i & 3), False)
        return carry

    group(x, y, True)
    lax.fori_loop(1, DEVICES // 8, step, 0)


def spectral_kernel(
    deposit, thermal, table, analysis, synthesis, damping, wave_y,
    home,
    padded, field, forcing, outgoing, incoming, lines, solved, modes,
    arrivals, wide, turned, edge_lo, edge_hi, halo_lo, halo_hi, corners, plane_out, plane_in,
    load_sems, edge_send, edge_recv, send_sems, recv_sems, own_sems, back_send, back_recv, back_own, home_sems,
):
    row, col = lax.axis_index("row"), lax.axis_index("col")
    me = row * COLS + col
    barrier = pltpu.get_barrier_semaphore()

    def greet(r, c):
        pl.semaphore_signal(barrier, inc=1, device_id=(r, c), device_id_type=MESH)

    deposit_load = pltpu.make_async_copy(
        deposit, padded.at[pl.ds(1, CZ), pl.ds(8, CY), :], load_sems.at[0]
    )
    deposit_load.start()
    field_load = pltpu.make_async_copy(thermal, field, load_sems.at[1])
    field_load.start()
    for_partners(row, col, greet)
    deposit_load.wait()

    def smooth(levels, blocks):
        low, count = levels[0], len(blocks)
        step, stride = levels[1] - levels[0], blocks[1] - blocks[0]

        def block(n, carry):
            level = low + n // count * step
            start = pl.multiple_of((blocks[0] + n % count * stride) * 16, 16)
            window = pl.ds(start, 32)
            mixed = 0.5 * padded[level + 1, window, :] + 0.25 * (
                padded[level, window, :] + padded[level + 2, window, :]
            )
            mixed = 0.5 * mixed[8:24] + 0.25 * (mixed[7:23] + mixed[9:25])
            mixed = 0.5 * mixed + 0.25 * (pltpu.roll(mixed, 1, 1) + pltpu.roll(mixed, NX - 1, 1))
            total = field[level, pl.ds(start, 16), :] + mixed
            forcing[pl.ds(pl.multiple_of(level * CY + start, 16), 16), :] = total.astype(BF16)
            return carry

        lax.fori_loop(0, len(levels) * count, block, 0)

    inner, outer = range(1, CY // 16 - 1), (0, CY // 16 - 1)

    for z in range(CZ):
        edge_lo[z : z + 1, :] = padded[1 + z, 8:9, :]
        edge_hi[z : z + 1, :] = padded[1 + z, 7 + CY : 8 + CY, :]
    plane_out[0] = padded[1, 8 : 8 + CY, :].astype(BF16)
    plane_out[1] = padded[CZ, 8 : 8 + CY, :].astype(BF16)
    field_load.wait()
    smooth(range(QUAD, CZ - QUAD), inner)
    pl.semaphore_wait(barrier, DEVICES - 1)
    row_up, row_dn = lax.rem(row + 1, ROWS), lax.rem(row + ROWS - 1, ROWS)
    col_up, col_dn = lax.rem(col + 1, COLS), lax.rem(col + COLS - 1, COLS)
    top, low = pl.ds(CZ - 8, 8), pl.ds(0, 8)
    halo_copies = []
    for n, (src, dst, where) in enumerate((
        (edge_hi, halo_lo, (row_up, col)),
        (edge_lo, halo_hi, (row_dn, col)),
        (edge_hi.at[top], corners.at[0], (row_up, col_up)),
        (edge_lo.at[top], corners.at[1], (row_dn, col_up)),
        (edge_hi.at[low], corners.at[2], (row_up, col_dn)),
        (edge_lo.at[low], corners.at[3], (row_dn, col_dn)),
        (plane_out.at[1], plane_in.at[0], (row, col_up)),
        (plane_out.at[0], plane_in.at[1], (row, col_dn)),
    )):
        copy = pltpu.make_async_remote_copy(
            src, dst, edge_send.at[n], edge_recv.at[n], device_id=where, device_id_type=MESH
        )
        copy.start()
        halo_copies.append(copy)
    smooth(range(1, QUAD), inner)
    smooth(range(CZ - QUAD, CZ - 1), inner)
    for n in (0, 1):
        halo_copies[n].wait_recv()
    for z in range(CZ):
        padded[1 + z, 7:8, :] = halo_lo[z : z + 1, :]
        padded[1 + z, 8 + CY : 9 + CY, :] = halo_hi[z : z + 1, :]

    def along_x(part):
        def block(n, carry):
            k = pl.multiple_of(n * 512, 512)
            out = dot(
                table[pl.ds(k, 512), :], forcing[part * QUAD * CY : (part + 1) * QUAD * CY, :], ((1,), (1,))
            )
            for pair in range(QUAD // 2):
                both = [
                    out[:, z * CY : (z + 1) * CY].reshape(64, OWN, CY)
                    for z in (2 * pair, 2 * pair + 1)
                ]
                outgoing[part, pl.ds(n * 64, 64), pair * 16 : pair * 16 + 16, :] = jnp.concatenate(
                    both, axis=1
                ).astype(BF16)
            return carry

        lax.fori_loop(0, NX // 512, block, 0)

    def landing(part):
        return incoming.at[
            part,
            pl.ds(pl.multiple_of(col * MSG, MSG), MSG),
            pl.ds(pl.multiple_of(row * CY, CY), CY),
        ]

    def send(part):
        def one(r, c):
            pltpu.make_async_remote_copy(
                outgoing.at[part, r * COLS + c], landing(part), send_sems.at[part], recv_sems.at[part],
                device_id=(r, c), device_id_type=MESH,
            ).start()

        for_partners(row, col, one)
        own = pltpu.make_async_copy(outgoing.at[part, me], landing(part), own_sems.at[part])
        own.start()
        return own

    owns = {}
    for part in ORDER:
        if part == ORDER[2]:
            for copy in halo_copies[2:]:
                copy.wait_recv()
            below, above = plane_in[0].astype(F32), plane_in[1].astype(F32)
            has_below, has_above = col > 0, col < COLS - 1
            padded[0, 8 : 8 + CY, :] = jnp.where(has_below, below, 0.0)
            padded[CZ + 1, 8 : 8 + CY, :] = jnp.where(has_above, above, 0.0)
            padded[0, 7:8, :] = jnp.where(has_below, corners[0, 7:8, :], 0.0)
            padded[0, 8 + CY : 9 + CY, :] = jnp.where(has_below, corners[1, 7:8, :], 0.0)
            padded[CZ + 1, 7:8, :] = jnp.where(has_above, corners[2, 0:1, :], 0.0)
            padded[CZ + 1, 8 + CY : 9 + CY, :] = jnp.where(has_above, corners[3, 0:1, :], 0.0)
            smooth((0, CZ - 1), inner)
            smooth((0, CZ - 1), outer)
        levels = range(part * QUAD, (part + 1) * QUAD)
        smooth([z for z in levels if 0 < z < CZ - 1], outer)
        along_x(part)
        owns[part] = send(part)

    for part in ORDER:
        owns[part].wait()
        arrived = outgoing.at[part, pl.ds(0, DEVICES - 1)]
        pltpu.make_async_copy(arrived, arrived, recv_sems.at[part]).wait()

        def along_y(n, carry, part=part):
            rows = pl.ds(pl.multiple_of(n * 512, 512), 512)
            out = dot(incoming[part, rows, :], table[...], ((1,), (0,)))
            for tile in range(NY // LANES):
                lines[part, tile, rows, :] = out[:, tile * LANES : (tile + 1) * LANES]
            return carry

        lax.fori_loop(0, COLS * MSG // 512, along_y, 0)

    def solve(k, carry):
        wave = me * OWN + k
        folded = jnp.minimum(wave, NX - wave).astype(F32) * (2.0 * math.pi / NX)
        base = 1.0 + DIFFUSION * folded * folded

        every = pl.ds(k, COLS * QUAD, stride=OWN)
        for n in range(NY // 256):
            planes = jnp.concatenate(
                [
                    jnp.concatenate([lines[part, 2 * n + t, every, :] for t in range(2)], axis=1)
                    for part in range(PARTS)
                ],
                axis=0,
            ).astype(BF16)
            modal = dot(analysis[...], planes, ((1,), (0,)))
            denom = (base + DIFFUSION * wave_y[0:1, n * 256 : (n + 1) * 256]) + damping[...]
            scaled = (modal / denom).astype(BF16)
            modes[:, n * 256 : (n + 1) * 256] = dot(synthesis[...], scaled, ((1,), (0,))).astype(BF16)
        solved[k] = dot(modes[...], table[...], ((1,), (0,))).astype(BF16)
        return carry

    def piece(begin, end, r, c):
        return solved.at[
            pl.ds(begin, end - begin),
            pl.ds(pl.multiple_of(c * CZ, CZ), CZ),
            pl.ds(pl.multiple_of(r * CY, CY), CY),
        ]

    back_owns = []
    spans = list(enumerate(zip(PHASES[:-1], PHASES[1:])))
    for phase, (begin, end) in spans:
        lax.fori_loop(begin, end, solve, 0)
        place = arrivals.at[pl.ds(begin, end - begin), me]

        def give(r, c, phase=phase, begin=begin, end=end, place=place):
            pltpu.make_async_remote_copy(
                piece(begin, end, r, c), place, back_send.at[phase], back_recv.at[phase],
                device_id=(r, c), device_id_type=MESH,
            ).start()

        for_partners(row, col, give)
        own = pltpu.make_async_copy(piece(begin, end, row, col), place, back_own.at[phase])
        own.start()
        back_owns.append(own)

    def turn(k):
        def widen(n, carry):
            rows = pl.ds(pl.multiple_of(n * 32 * CZ, 32 * CZ), 32 * CZ)
            wide[rows, :] = arrivals[k, pl.ds(n * 32, 32)].astype(F32).reshape(32 * CZ, CY)
            return carry

        lax.fori_loop(0, DEVICES // 32, widen, 0)
        for z in range(CZ):
            turned[k % 2, z] = wide[pl.ds(z, DEVICES, stride=CZ), :].T.astype(BF16)
        return pltpu.make_async_copy(
            turned.at[k % 2], home.at[:, :, pl.ds(k * DEVICES, DEVICES)], home_sems.at[k]
        )

    homes = []
    for phase, (begin, end) in spans:
        back_owns[phase].wait()
        arrived = arrivals.at[pl.ds(begin, end - begin), pl.ds(0, DEVICES - 1)]
        pltpu.make_async_copy(arrived, arrived, back_recv.at[phase]).wait()
        for k in range(begin, end):
            if k >= 2:
                homes[k - 2].wait()
            homes.append(turn(k))
            homes[k].start()
    for phase, (begin, end) in spans:
        sent = arrivals.at[pl.ds(begin, end - begin), pl.ds(0, DEVICES - 1)]
        pltpu.make_async_copy(sent, sent, back_send.at[phase]).wait()
    for copy in homes[-2:]:
        copy.wait()
    for part in range(PARTS):
        sent = outgoing.at[part, pl.ds(0, DEVICES - 1)]
        pltpu.make_async_copy(sent, sent, send_sems.at[part]).wait()
    for copy in halo_copies:
        copy.wait_send()


def spectral_step(deposit, thermal, table, analysis, synthesis, damping, wave_y):
    any_space, vmem = pl.BlockSpec(memory_space=pl.ANY), pl.BlockSpec(memory_space=pltpu.VMEM)
    return pl.pallas_call(
        spectral_kernel,
        out_shape=jax.ShapeDtypeStruct((CZ, CY, NX), BF16),
        in_specs=[any_space, any_space, vmem, vmem, vmem, vmem, vmem],
        out_specs=any_space,
        scratch_shapes=[
            pltpu.VMEM((CZ + 2, CY + 16, NX), F32),
            pltpu.VMEM((CZ, CY, NX), F32),
            pltpu.VMEM((CZ * CY, NX), BF16),
            pltpu.VMEM((PARTS, DEVICES, MSG, CY), BF16),
            pltpu.VMEM((PARTS, COLS * MSG, NY), BF16),
            pltpu.VMEM((PARTS, NY // LANES, COLS * MSG, LANES), F32),
            pltpu.VMEM((OWN, NZ, NY), BF16),
            pltpu.VMEM((NZ, NY), BF16),
            pltpu.VMEM((OWN, DEVICES, CZ, CY), BF16),
            pltpu.VMEM((DEVICES * CZ, CY), F32),
            pltpu.VMEM((2, CZ, CY, DEVICES), BF16),
            pltpu.VMEM((CZ, NX), F32),
            pltpu.VMEM((CZ, NX), F32),
            pltpu.VMEM((CZ, NX), F32),
            pltpu.VMEM((CZ, NX), F32),
            pltpu.VMEM((4, 8, NX), F32),
            pltpu.VMEM((2, CY, NX), BF16),
            pltpu.VMEM((2, CY, NX), BF16),
            pltpu.SemaphoreType.DMA((2,)),
            pltpu.SemaphoreType.DMA((8,)),
            pltpu.SemaphoreType.DMA((8,)),
            pltpu.SemaphoreType.DMA((PARTS,)),
            pltpu.SemaphoreType.DMA((PARTS,)),
            pltpu.SemaphoreType.DMA((PARTS,)),
            pltpu.SemaphoreType.DMA((len(PHASES) - 1,)),
            pltpu.SemaphoreType.DMA((len(PHASES) - 1,)),
            pltpu.SemaphoreType.DMA((len(PHASES) - 1,)),
            pltpu.SemaphoreType.DMA((OWN,)),
        ],
        compiler_params=pltpu.CompilerParams(
            collective_id=0, has_side_effects=True, vmem_limit_bytes=60 * 2**20
        ),
        name="spectral_step",
    )(deposit, thermal, table, analysis, synthesis, damping, wave_y)


def home_kernel(home, table, out):
    for x in range(0, NX, 256):
        out[:, x : x + 256] = dot(home[...], table[:, x : x + 256], ((1,), (0,)))


def home_step(home, table):
    rows = QUAD * CY
    out = pl.pallas_call(
        home_kernel,
        grid=(CZ // QUAD,),
        out_shape=jax.ShapeDtypeStruct((CZ * CY, NX), F32),
        in_specs=[
            pl.BlockSpec((rows, NX), lambda i: (i, 0)),
            pl.BlockSpec((NX, NX), lambda i: (0, 0)),
        ],
        out_specs=pl.BlockSpec((rows, NX), lambda i: (i, 0)),
        compiler_params=pltpu.CompilerParams(vmem_limit_bytes=50 * 2**20),
        name="home_step",
    )(home.reshape(CZ * CY, NX), table)
    return out.reshape(CZ, CY, NX)


def deposit_kernel(first, last, keys, energy, out, key_rows, energy_rows):
    level, rows = pl.program_id(0), keys.shape[0]

    @pl.when(level == 0)
    def _():
        key_rows[0:rows, :] = keys[...]
        energy_rows[0:rows, :] = energy[...]
        key_rows[rows:, :] = jnp.full((WINDOW, LANES), GROUPS * CY * LANES, jnp.int32)
        energy_rows[rows:, :] = jnp.zeros((WINDOW, LANES), F32)

    lane = lax.broadcasted_iota(jnp.int32, (LANES, LANES), 0).astype(BF16)
    one, nil = jnp.ones((LANES, LANES), BF16), jnp.zeros((LANES, LANES), BF16)

    def tile(group, start):
        chosen, high, rest = [], [], []
        for n in range(WINDOW):
            key, heat = key_rows[pl.ds(start + n, 1), :], energy_rows[pl.ds(start + n, 1), :]
            hit = lane == (key & (LANES - 1)).astype(F32).astype(BF16)
            top = heat.astype(BF16)
            high.append(jnp.where(hit, top, nil))
            rest.append(jnp.where(hit, (heat - top.astype(F32)).astype(BF16), nil))
            line = (key >> 7) - group * CY
            line = jnp.where((line >= 0) & (line < CY), line, -1).astype(F32).astype(BF16)
            chosen.append(jnp.where(lane == line, one, nil))
        weights = jnp.concatenate(
            [jnp.concatenate(high, axis=1), jnp.concatenate(rest, axis=1)], axis=0
        )
        sums = dot(jnp.concatenate(chosen, axis=1), weights, ((1,), (1,)))
        return sums[:, :LANES] + sums[:, LANES:]

    per_level = NX // LANES
    starts = [first[level * per_level + n] for n in range(per_level)]
    for n, start in enumerate(starts):
        out[0, :, n * LANES : (n + 1) * LANES] = tile(level * per_level + n, start)
    for n, start in enumerate(starts):
        group = level * per_level + n

        def further(w, c, n=n, group=group, start=start):
            out[0, :, n * LANES : (n + 1) * LANES] += tile(group, start + w * WINDOW)
            return c

        lax.fori_loop(1, (last[group] - start + WINDOW - 1) // WINDOW, further, 0)


def deposit_step(location, energy, tally):
    slots = energy.shape[0]
    live = jnp.arange(slots, dtype=jnp.int32) < tally[0]
    x = location[0]
    key = ((location[2] * (NX // LANES) + x // LANES) * CY + location[1]) * LANES + x % LANES
    key = jnp.where(live, key, GROUPS * CY * LANES)
    energy = jnp.where(live, energy, 0.0)
    key, energy = lax.sort((key, energy), num_keys=1, is_stable=False)
    key, energy = key.reshape(-1, LANES), energy.reshape(-1, LANES)
    group = jnp.arange(GROUPS, dtype=jnp.int32)[:, None] * (CY * LANES)
    first = jnp.sum((key[:, LANES - 1] < group).astype(jnp.int32), axis=1)
    last = jnp.sum((key[:, 0] < group + CY * LANES).astype(jnp.int32), axis=1)
    smem, vmem = pl.BlockSpec(memory_space=pltpu.SMEM), pl.BlockSpec(memory_space=pltpu.VMEM)
    return pl.pallas_call(
        deposit_kernel,
        out_shape=jax.ShapeDtypeStruct((CZ, CY, NX), F32),
        grid=(CZ,),
        in_specs=[smem, smem, vmem, vmem],
        out_specs=pl.BlockSpec((1, CY, NX), lambda z: (z, 0, 0)),
        scratch_shapes=[
            pltpu.VMEM((slots // LANES + WINDOW, LANES), jnp.int32),
            pltpu.VMEM((slots // LANES + WINDOW, LANES), F32),
        ],
        compiler_params=pltpu.CompilerParams(vmem_limit_bytes=50 * 2**20),
        name="deposit_step",
    )(first, last, key, energy)


def body(thermal, location, energy, tally, decay, analysis, synthesis):
    deposit = deposit_step(location, energy, tally)
    table = jnp.asarray(cas_table(NX))
    analysis = analysis.reshape(NZ, COLS, PARTS, QUAD).transpose(0, 2, 1, 3).reshape(NZ, NZ)
    index = np.arange(NY)
    wave_y = ((np.minimum(index, NY - index) * (2.0 * math.pi / NY)) ** 2).astype(np.float32)
    home = spectral_step(
        deposit, thermal, table, analysis, synthesis, decay[:, None], jnp.asarray(wave_y)[None, :]
    )
    ordered = cas_table(NX).reshape(DEVICES, OWN, NX).transpose(1, 0, 2).reshape(NX, NX)
    return home_step(home, jnp.asarray(ordered))


def solution(mesh):
    in_specs = (
        P("col", "row", None),
        P(None, ("row", "col")),
        P(("row", "col")),
        P(("row", "col")),
        P(),
        P(),
        P(),
    )
    return jax.shard_map(
        body, mesh=mesh, in_specs=in_specs, out_specs=P("col", "row", None), check_vma=False
    )
```

```python
import functools
import math

import jax
import jax.numpy as jnp
import ml_dtypes
import numpy as np
from jax import lax
from jax.experimental import pallas as pl
from jax.experimental.pallas import tpu as pltpu
from jax.sharding import PartitionSpec as P

DIFFUSION = 0.1
MESH = pl.DeviceIdType.MESH
F32 = jnp.float32
BF16 = jnp.bfloat16
ROWS, COLS = 8, 16
DEVICES = ROWS * COLS
NX = NY = 1024
NZ = 256
CY, CZ = 128, 16
OWN = NX // DEVICES
PARTS = 4
QUAD = CZ // PARTS
MSG = QUAD * OWN
PHASES = (0, 1, 3, 5, 7, 8)
ORDER = (1, 2, 0, 3)
LANES = 128
WINDOW = 6
GROUPS = CZ * NX // LANES


def cas_table(length):
    index = np.arange(length)
    angle = (index[:, None] * index[None, :] % length) * (2.0 * math.pi / length)
    return ((np.cos(angle) + np.sin(angle)) / math.sqrt(length)).astype(ml_dtypes.bfloat16)


def dot(a, b, contract):
    return lax.dot_general(a, b, (contract, ((), ())), preferred_element_type=F32)


def for_partners(row, col, act):
    x, y, z, core = row >> 1, (col >> 1) & 3, ((col >> 3) << 1) + (row & 1), col & 1
    depths = [(z + t) & 3 for t in range(4)]
    z_row = [depth & 1 for depth in depths]
    z_col = [((depth >> 1) << 3) + c for depth in depths for c in (core, core ^ 1)]

    def group(x, y, skip):
        for t in range(4):
            r = (((x + t) & 3) << 1) + z_row[t]
            near = ((y + t) & 3) << 1
            for c in range(2):
                if t or c or not skip:
                    act(r, z_col[2 * t + c] + near)

    def step(i, carry):
        group(x + (i >> 2), y + (i & 3), False)
        return carry

    group(x, y, True)
    lax.fori_loop(1, DEVICES // 8, step, 0)


def spectral_kernel(
    deposit, thermal, table, analysis, synthesis, decay, wave_y,
    home,
    ordered, damping,
    padded, field, forcing, outgoing, incoming, lines, solved, modes,
    arrivals, wide, turned, edge_lo, edge_hi, halo_lo, halo_hi, corners, plane_out, plane_in,
    load_sems, edge_send, edge_recv, send_sems, recv_sems, own_sems, back_send, back_recv, back_own, home_sems,
):
    row, col = lax.axis_index("row"), lax.axis_index("col")
    me = row * COLS + col
    barrier = pltpu.get_barrier_semaphore()

    def greet(r, c):
        pl.semaphore_signal(barrier, inc=1, device_id=(r, c), device_id_type=MESH)

    deposit_load = pltpu.make_async_copy(
        deposit, padded.at[pl.ds(1, CZ), pl.ds(8, CY), :], load_sems.at[0]
    )
    deposit_load.start()
    field_load = pltpu.make_async_copy(thermal, field, load_sems.at[1])
    for_partners(row, col, greet)
    field_load.start()
    deposit_load.wait()

    def smooth(levels, blocks):
        low, count = levels[0], len(blocks)
        step, stride = levels[1] - levels[0], blocks[1] - blocks[0]

        def block(n, carry):
            level = low + n // count * step
            start = pl.multiple_of((blocks[0] + n % count * stride) * 16, 16)
            window = pl.ds(start, 32)
            mixed = 0.5 * padded[level + 1, window, :] + 0.25 * (
                padded[level, window, :] + padded[level + 2, window, :]
            )
            mixed = 0.5 * mixed[8:24] + 0.25 * (mixed[7:23] + mixed[9:25])
            mixed = 0.5 * mixed + 0.25 * (pltpu.roll(mixed, 1, 1) + pltpu.roll(mixed, NX - 1, 1))
            total = field[level, pl.ds(start, 16), :] + mixed
            forcing[pl.ds(pl.multiple_of(level * CY + start, 16), 16), :] = total.astype(BF16)
            return carry

        lax.fori_loop(0, len(levels) * count, block, 0)

    inner, outer = range(1, CY // 16 - 1), (0, CY // 16 - 1)

    place = lax.broadcasted_iota(jnp.int32, (NZ, NZ), 1)
    level = ((place >> 2) & (COLS - 1)) * CZ + (place >> 6) * QUAD + (place & (QUAD - 1))
    moved = (lax.broadcasted_iota(jnp.int32, (NZ, NZ), 0) == level).astype(F32).astype(BF16)
    ordered[...] = dot(analysis[...], moved, ((1,), (0,))).astype(BF16)
    damping[...] = jnp.broadcast_to(decay[...], (LANES, NZ)).T

    for z in range(CZ):
        edge_lo[z : z + 1, :] = padded[1 + z, 8:9, :]
        edge_hi[z : z + 1, :] = padded[1 + z, 7 + CY : 8 + CY, :]
    plane_out[0] = padded[1, 8 : 8 + CY, :].astype(BF16)
    plane_out[1] = padded[CZ, 8 : 8 + CY, :].astype(BF16)
    pl.semaphore_wait(barrier, DEVICES - 1)
    row_up, row_dn = lax.rem(row + 1, ROWS), lax.rem(row + ROWS - 1, ROWS)
    col_up, col_dn = lax.rem(col + 1, COLS), lax.rem(col + COLS - 1, COLS)
    top, low = pl.ds(CZ - 8, 8), pl.ds(0, 8)
    halo_copies = []
    for n, (src, dst, where) in enumerate((
        (edge_hi, halo_lo, (row_up, col)),
        (edge_lo, halo_hi, (row_dn, col)),
        (edge_hi.at[top], corners.at[0], (row_up, col_up)),
        (edge_lo.at[top], corners.at[1], (row_dn, col_up)),
        (edge_hi.at[low], corners.at[2], (row_up, col_dn)),
        (edge_lo.at[low], corners.at[3], (row_dn, col_dn)),
        (plane_out.at[1], plane_in.at[0], (row, col_up)),
        (plane_out.at[0], plane_in.at[1], (row, col_dn)),
    )):
        copy = pltpu.make_async_remote_copy(
            src, dst, edge_send.at[n], edge_recv.at[n], device_id=where, device_id_type=MESH
        )
        copy.start()
        halo_copies.append(copy)
    field_load.wait()
    smooth(range(QUAD, CZ - QUAD), inner)
    for n in (0, 1):
        halo_copies[n].wait_recv()
    for z in range(CZ):
        padded[1 + z, 7:8, :] = halo_lo[z : z + 1, :]
        padded[1 + z, 8 + CY : 9 + CY, :] = halo_hi[z : z + 1, :]

    def along_x(part):
        def block(n, carry):
            k = pl.multiple_of(n * 512, 512)
            out = dot(
                table[pl.ds(k, 512), :], forcing[part * QUAD * CY : (part + 1) * QUAD * CY, :], ((1,), (1,))
            )
            for pair in range(QUAD // 2):
                both = [
                    out[:, z * CY : (z + 1) * CY].reshape(64, OWN, CY)
                    for z in (2 * pair, 2 * pair + 1)
                ]
                outgoing[part, pl.ds(n * 64, 64), pair * 16 : pair * 16 + 16, :] = jnp.concatenate(
                    both, axis=1
                ).astype(BF16)
            return carry

        lax.fori_loop(0, NX // 512, block, 0)

    def landing(part):
        return incoming.at[
            part,
            pl.ds(pl.multiple_of(col * MSG, MSG), MSG),
            pl.ds(pl.multiple_of(row * CY, CY), CY),
        ]

    def send(part):
        def one(r, c):
            pltpu.make_async_remote_copy(
                outgoing.at[part, r * COLS + c], landing(part), send_sems.at[part], recv_sems.at[part],
                device_id=(r, c), device_id_type=MESH,
            ).start()

        for_partners(row, col, one)
        own = pltpu.make_async_copy(outgoing.at[part, me], landing(part), own_sems.at[part])
        own.start()
        return own

    owns = {}
    for part in ORDER:
        if part == ORDER[2]:
            for copy in halo_copies[2:]:
                copy.wait_recv()
            below, above = plane_in[0].astype(F32), plane_in[1].astype(F32)
            has_below, has_above = col > 0, col < COLS - 1
            padded[0, 8 : 8 + CY, :] = jnp.where(has_below, below, 0.0)
            padded[CZ + 1, 8 : 8 + CY, :] = jnp.where(has_above, above, 0.0)
            padded[0, 7:8, :] = jnp.where(has_below, corners[0, 7:8, :], 0.0)
            padded[0, 8 + CY : 9 + CY, :] = jnp.where(has_below, corners[1, 7:8, :], 0.0)
            padded[CZ + 1, 7:8, :] = jnp.where(has_above, corners[2, 0:1, :], 0.0)
            padded[CZ + 1, 8 + CY : 9 + CY, :] = jnp.where(has_above, corners[3, 0:1, :], 0.0)
            smooth((0, CZ - 1), inner)
            smooth((0, CZ - 1), outer)
            smooth(range(1, QUAD), inner)
            smooth(range(CZ - QUAD, CZ - 1), inner)
        levels = range(part * QUAD, (part + 1) * QUAD)
        smooth([z for z in levels if 0 < z < CZ - 1], outer)
        along_x(part)
        owns[part] = send(part)

    for part in ORDER:
        owns[part].wait()
        arrived = outgoing.at[part, pl.ds(0, DEVICES - 1)]
        pltpu.make_async_copy(arrived, arrived, recv_sems.at[part]).wait()

        def along_y(n, carry, part=part):
            rows = pl.ds(pl.multiple_of(n * 512, 512), 512)
            out = dot(incoming[part, rows, :], table[...], ((1,), (0,)))
            for tile in range(NY // LANES):
                lines[part, tile, rows, :] = out[:, tile * LANES : (tile + 1) * LANES]
            return carry

        lax.fori_loop(0, COLS * MSG // 512, along_y, 0)

    def solve(k, carry):
        wave = me * OWN + k
        folded = jnp.minimum(wave, NX - wave).astype(F32) * (2.0 * math.pi / NX)
        base = 1.0 + DIFFUSION * folded * folded

        every = pl.ds(k, COLS * QUAD, stride=OWN)
        for n in range(NY // 256):
            planes = jnp.concatenate(
                [
                    jnp.concatenate([lines[part, 2 * n + t, every, :] for t in range(2)], axis=1)
                    for part in range(PARTS)
                ],
                axis=0,
            ).astype(BF16)
            modal = dot(ordered[...], planes, ((1,), (0,)))
            denom = (base + DIFFUSION * wave_y[0:1, n * 256 : (n + 1) * 256]) + damping[:, 0:1]
            scaled = (modal / denom).astype(BF16)
            modes[:, n * 256 : (n + 1) * 256] = dot(synthesis[...], scaled, ((1,), (0,))).astype(BF16)
        solved[k] = dot(modes[...], table[...], ((1,), (0,))).astype(BF16)
        return carry

    def piece(begin, end, r, c):
        return solved.at[
            pl.ds(begin, end - begin),
            pl.ds(pl.multiple_of(c * CZ, CZ), CZ),
            pl.ds(pl.multiple_of(r * CY, CY), CY),
        ]

    back_owns = []
    spans = list(enumerate(zip(PHASES[:-1], PHASES[1:])))
    for phase, (begin, end) in spans:
        lax.fori_loop(begin, end, solve, 0)
        place = arrivals.at[pl.ds(begin, end - begin), me]

        def give(r, c, phase=phase, begin=begin, end=end, place=place):
            pltpu.make_async_remote_copy(
                piece(begin, end, r, c), place, back_send.at[phase], back_recv.at[phase],
                device_id=(r, c), device_id_type=MESH,
            ).start()

        for_partners(row, col, give)
        own = pltpu.make_async_copy(piece(begin, end, row, col), place, back_own.at[phase])
        own.start()
        back_owns.append(own)

    def turn(k):
        def widen(n, carry):
            rows = pl.ds(pl.multiple_of(n * 32 * CZ, 32 * CZ), 32 * CZ)
            wide[rows, :] = arrivals[k, pl.ds(n * 32, 32)].astype(F32).reshape(32 * CZ, CY)
            return carry

        lax.fori_loop(0, DEVICES // 32, widen, 0)
        for z in range(CZ):
            turned[k % 2, z] = wide[pl.ds(z, DEVICES, stride=CZ), :].T.astype(BF16)
        return pltpu.make_async_copy(
            turned.at[k % 2], home.at[:, :, pl.ds(k * DEVICES, DEVICES)], home_sems.at[k]
        )

    homes = []
    for phase, (begin, end) in spans:
        back_owns[phase].wait()
        arrived = arrivals.at[pl.ds(begin, end - begin), pl.ds(0, DEVICES - 1)]
        pltpu.make_async_copy(arrived, arrived, back_recv.at[phase]).wait()
        for k in range(begin, end):
            if k >= 2:
                homes[k - 2].wait()
            homes.append(turn(k))
            homes[k].start()
    for phase, (begin, end) in spans:
        sent = arrivals.at[pl.ds(begin, end - begin), pl.ds(0, DEVICES - 1)]
        pltpu.make_async_copy(sent, sent, back_send.at[phase]).wait()
    for copy in homes[-2:]:
        copy.wait()
    for part in range(PARTS):
        sent = outgoing.at[part, pl.ds(0, DEVICES - 1)]
        pltpu.make_async_copy(sent, sent, send_sems.at[part]).wait()
    for copy in halo_copies:
        copy.wait_send()


def spectral_step(deposit, thermal, table, analysis, synthesis, decay, wave_y):
    any_space, vmem = pl.BlockSpec(memory_space=pl.ANY), pl.BlockSpec(memory_space=pltpu.VMEM)
    return pl.pallas_call(
        spectral_kernel,
        out_shape=jax.ShapeDtypeStruct((CZ, CY, NX), BF16),
        in_specs=[any_space, any_space, vmem, vmem, vmem, vmem, vmem],
        out_specs=any_space,
        scratch_shapes=[
            pltpu.VMEM((NZ, NZ), BF16),
            pltpu.VMEM((NZ, LANES), F32),
            pltpu.VMEM((CZ + 2, CY + 16, NX), F32),
            pltpu.VMEM((CZ, CY, NX), F32),
            pltpu.VMEM((CZ * CY, NX), BF16),
            pltpu.VMEM((PARTS, DEVICES, MSG, CY), BF16),
            pltpu.VMEM((PARTS, COLS * MSG, NY), BF16),
            pltpu.VMEM((PARTS, NY // LANES, COLS * MSG, LANES), F32),
            pltpu.VMEM((OWN, NZ, NY), BF16),
            pltpu.VMEM((NZ, NY), BF16),
            pltpu.VMEM((OWN, DEVICES, CZ, CY), BF16),
            pltpu.VMEM((DEVICES * CZ, CY), F32),
            pltpu.VMEM((2, CZ, CY, DEVICES), BF16),
            pltpu.VMEM((CZ, NX), F32),
            pltpu.VMEM((CZ, NX), F32),
            pltpu.VMEM((CZ, NX), F32),
            pltpu.VMEM((CZ, NX), F32),
            pltpu.VMEM((4, 8, NX), F32),
            pltpu.VMEM((2, CY, NX), BF16),
            pltpu.VMEM((2, CY, NX), BF16),
            pltpu.SemaphoreType.DMA((2,)),
            pltpu.SemaphoreType.DMA((8,)),
            pltpu.SemaphoreType.DMA((8,)),
            pltpu.SemaphoreType.DMA((PARTS,)),
            pltpu.SemaphoreType.DMA((PARTS,)),
            pltpu.SemaphoreType.DMA((PARTS,)),
            pltpu.SemaphoreType.DMA((len(PHASES) - 1,)),
            pltpu.SemaphoreType.DMA((len(PHASES) - 1,)),
            pltpu.SemaphoreType.DMA((len(PHASES) - 1,)),
            pltpu.SemaphoreType.DMA((OWN,)),
        ],
        compiler_params=pltpu.CompilerParams(
            collective_id=0, has_side_effects=True, vmem_limit_bytes=60 * 2**20
        ),
        name="spectral_step",
    )(deposit, thermal, table, analysis, synthesis, decay, wave_y)


def home_kernel(home, table, out):
    for x in range(0, NX, 256):
        out[:, x : x + 256] = dot(home[...], table[:, x : x + 256], ((1,), (0,)))


def home_step(home, table):
    rows = QUAD * CY
    out = pl.pallas_call(
        home_kernel,
        grid=(CZ // QUAD,),
        out_shape=jax.ShapeDtypeStruct((CZ * CY, NX), F32),
        in_specs=[
            pl.BlockSpec((rows, NX), lambda i: (i, 0)),
            pl.BlockSpec((NX, NX), lambda i: (0, 0)),
        ],
        out_specs=pl.BlockSpec((rows, NX), lambda i: (i, 0)),
        compiler_params=pltpu.CompilerParams(vmem_limit_bytes=50 * 2**20),
        name="home_step",
    )(home.reshape(CZ * CY, NX), table)
    return out.reshape(CZ, CY, NX)


def deposit_kernel(first, last, keys, energy, out, key_rows, energy_rows):
    level, rows = pl.program_id(0), keys.shape[0]

    @pl.when(level == 0)
    def _():
        key_rows[0:rows, :] = keys[...]
        energy_rows[0:rows, :] = energy[...]
        key_rows[rows:, :] = jnp.full((WINDOW, LANES), GROUPS * CY * LANES, jnp.int32)
        energy_rows[rows:, :] = jnp.zeros((WINDOW, LANES), F32)

    lane = lax.broadcasted_iota(jnp.int32, (LANES, LANES), 0).astype(BF16)
    one, nil = jnp.ones((LANES, LANES), BF16), jnp.zeros((LANES, LANES), BF16)

    def tile(group, start):
        chosen, weights = [], []
        for n in range(WINDOW):
            key, heat = key_rows[pl.ds(start + n, 1), :], energy_rows[pl.ds(start + n, 1), :]
            hit = lane == (key & (LANES - 1)).astype(F32).astype(BF16)
            weights.append(jnp.where(hit, heat.astype(BF16), nil))
            line = (key >> 7) - group * CY
            line = jnp.where((line >= 0) & (line < CY), line, -1).astype(F32).astype(BF16)
            chosen.append(jnp.where(lane == line, one, nil))
        return dot(jnp.concatenate(chosen, axis=1), jnp.concatenate(weights, axis=1), ((1,), (1,)))

    per_level = NX // LANES
    starts = [first[level * per_level + n] for n in range(per_level)]
    for n, start in enumerate(starts):
        out[0, :, n * LANES : (n + 1) * LANES] = tile(level * per_level + n, start)
    for n, start in enumerate(starts):
        group = level * per_level + n

        def further(w, c, n=n, group=group, start=start):
            out[0, :, n * LANES : (n + 1) * LANES] += tile(group, start + w * WINDOW)
            return c

        lax.fori_loop(1, (last[group] - start + WINDOW - 1) // WINDOW, further, 0)


def deposit_step(location, energy, tally):
    slots = energy.shape[0]
    live = jnp.arange(slots, dtype=jnp.int32) < tally[0]
    x = location[0]
    key = ((location[2] * (NX // LANES) + x // LANES) * CY + location[1]) * LANES + x % LANES
    key = jnp.where(live, key, GROUPS * CY * LANES)
    key, energy = lax.sort((key, energy), num_keys=1, is_stable=False)
    key, energy = key.reshape(-1, LANES), energy.reshape(-1, LANES)
    group = jnp.arange(GROUPS, dtype=jnp.int32)[:, None] * (CY * LANES)
    first = jnp.sum((key[:, LANES - 1] < group).astype(jnp.int32), axis=1)
    last = jnp.sum((key[:, 0] < group + CY * LANES).astype(jnp.int32), axis=1)
    smem, vmem = pl.BlockSpec(memory_space=pltpu.SMEM), pl.BlockSpec(memory_space=pltpu.VMEM)
    return pl.pallas_call(
        deposit_kernel,
        out_shape=jax.ShapeDtypeStruct((CZ, CY, NX), F32),
        grid=(CZ,),
        in_specs=[smem, smem, vmem, vmem],
        out_specs=pl.BlockSpec((1, CY, NX), lambda z: (z, 0, 0)),
        scratch_shapes=[
            pltpu.VMEM((slots // LANES + WINDOW, LANES), jnp.int32),
            pltpu.VMEM((slots // LANES + WINDOW, LANES), F32),
        ],
        compiler_params=pltpu.CompilerParams(vmem_limit_bytes=50 * 2**20),
        name="deposit_step",
    )(first, last, key, energy)


def body(thermal, location, energy, tally, decay, analysis, synthesis):
    deposit = deposit_step(location, energy, tally)
    table = jnp.asarray(cas_table(NX))
    index = np.arange(NY)
    wave_y = ((np.minimum(index, NY - index) * (2.0 * math.pi / NY)) ** 2).astype(np.float32)
    home = spectral_step(
        deposit, thermal, table, analysis, synthesis, decay[None, :], jnp.asarray(wave_y)[None, :]
    )
    ordered = cas_table(NX).reshape(DEVICES, OWN, NX).transpose(1, 0, 2).reshape(NX, NX)
    return home_step(home, jnp.asarray(ordered))


def solution(mesh):
    in_specs = (
        P("col", "row", None),
        P(None, ("row", "col")),
        P(("row", "col")),
        P(("row", "col")),
        P(),
        P(),
        P(),
    )
    return jax.shard_map(
        body, mesh=mesh, in_specs=in_specs, out_specs=P("col", "row", None), check_vma=False
    )
```

```python
import functools
import math

import jax
import jax.numpy as jnp
import ml_dtypes
import numpy as np
from jax import lax
from jax.experimental import pallas as pl
from jax.experimental.pallas import tpu as pltpu
from jax.sharding import PartitionSpec as P

DIFFUSION = 0.1
MESH = pl.DeviceIdType.MESH
F32 = jnp.float32
BF16 = jnp.bfloat16
ROWS, COLS = 8, 16
DEVICES = ROWS * COLS
NX = NY = 1024
NZ = 256
CY, CZ = 128, 16
OWN = NX // DEVICES
PARTS = 4
QUAD = CZ // PARTS
MSG = QUAD * OWN
PHASES = (0, 1, 2, 4, 6, 7, 8)
ORDER = (1, 2, 0, 3)
LANES = 128
WINDOW = 6
GROUPS = CZ * NX // LANES


def cas_table(length):
    index = np.arange(length)
    angle = (index[:, None] * index[None, :] % length) * (2.0 * math.pi / length)
    return ((np.cos(angle) + np.sin(angle)) / math.sqrt(length)).astype(ml_dtypes.bfloat16)


def dot(a, b, contract):
    return lax.dot_general(a, b, (contract, ((), ())), preferred_element_type=F32)


def for_partners(row, col, act):
    x, y, z, core = row >> 1, (col >> 1) & 3, ((col >> 3) << 1) + (row & 1), col & 1
    depths = [(z + t) & 3 for t in range(4)]
    z_row = [depth & 1 for depth in depths]
    z_col = [((depth >> 1) << 3) + c for depth in depths for c in (core, core ^ 1)]

    def group(x, y, skip):
        for t in range(4):
            r = (((x + t) & 3) << 1) + z_row[t]
            near = ((y + t) & 3) << 1
            for c in range(2):
                if t or c or not skip:
                    act(r, z_col[2 * t + c] + near)

    def step(i, carry):
        group(x + (i >> 2), y + (i & 3), False)
        return carry

    group(x, y, True)
    lax.fori_loop(1, DEVICES // 8, step, 0)


def spectral_kernel(
    deposit, thermal, table, analysis, synthesis, decay, wave_y,
    home,
    ordered, damping,
    padded, field, forcing, outgoing, incoming, lines, solved, modes,
    arrivals, wide, turned, edge_lo, edge_hi, halo_lo, halo_hi, corners, plane_out, plane_in,
    load_sems, edge_send, edge_recv, send_sems, recv_sems, own_sems, back_send, back_recv, back_own, home_sems,
):
    row, col = lax.axis_index("row"), lax.axis_index("col")
    me = row * COLS + col
    barrier = pltpu.get_barrier_semaphore()

    def greet(r, c):
        pl.semaphore_signal(barrier, inc=1, device_id=(r, c), device_id_type=MESH)

    deposit_load = pltpu.make_async_copy(
        deposit, padded.at[pl.ds(1, CZ), pl.ds(8, CY), :], load_sems.at[0]
    )
    deposit_load.start()
    field_load = pltpu.make_async_copy(thermal, field, load_sems.at[1])
    for_partners(row, col, greet)
    field_load.start()
    deposit_load.wait()

    def smooth(levels, blocks):
        low, count = levels[0], len(blocks)
        step, stride = levels[1] - levels[0], blocks[1] - blocks[0]

        def block(n, carry):
            level = low + n // count * step
            start = pl.multiple_of((blocks[0] + n % count * stride) * 16, 16)
            window = pl.ds(start, 32)
            mixed = 0.5 * padded[level + 1, window, :] + 0.25 * (
                padded[level, window, :] + padded[level + 2, window, :]
            )
            mixed = 0.5 * mixed[8:24] + 0.25 * (mixed[7:23] + mixed[9:25])
            mixed = 0.5 * mixed + 0.25 * (pltpu.roll(mixed, 1, 1) + pltpu.roll(mixed, NX - 1, 1))
            total = field[level, pl.ds(start, 16), :] + mixed
            forcing[pl.ds(pl.multiple_of(level * CY + start, 16), 16), :] = total.astype(BF16)
            return carry

        lax.fori_loop(0, len(levels) * count, block, 0)

    inner, outer = range(1, CY // 16 - 1), (0, CY // 16 - 1)

    place = lax.broadcasted_iota(jnp.int32, (NZ, NZ), 1)
    level = ((place >> 2) & (COLS - 1)) * CZ + (place >> 6) * QUAD + (place & (QUAD - 1))
    moved = (lax.broadcasted_iota(jnp.int32, (NZ, NZ), 0) == level).astype(F32).astype(BF16)
    ordered[...] = dot(analysis[...], moved, ((1,), (0,))).astype(BF16)
    damping[...] = jnp.broadcast_to(decay[...], (LANES, NZ)).T

    for z in range(CZ):
        edge_lo[z : z + 1, :] = padded[1 + z, 8:9, :]
        edge_hi[z : z + 1, :] = padded[1 + z, 7 + CY : 8 + CY, :]
    plane_out[0] = padded[1, 8 : 8 + CY, :].astype(BF16)
    plane_out[1] = padded[CZ, 8 : 8 + CY, :].astype(BF16)
    pl.semaphore_wait(barrier, DEVICES - 1)
    row_up, row_dn = lax.rem(row + 1, ROWS), lax.rem(row + ROWS - 1, ROWS)
    col_up, col_dn = lax.rem(col + 1, COLS), lax.rem(col + COLS - 1, COLS)
    top, low = pl.ds(CZ - 8, 8), pl.ds(0, 8)
    halo_copies = []
    for n, (src, dst, where) in enumerate((
        (edge_hi, halo_lo, (row_up, col)),
        (edge_lo, halo_hi, (row_dn, col)),
        (edge_hi.at[top], corners.at[0], (row_up, col_up)),
        (edge_lo.at[top], corners.at[1], (row_dn, col_up)),
        (edge_hi.at[low], corners.at[2], (row_up, col_dn)),
        (edge_lo.at[low], corners.at[3], (row_dn, col_dn)),
        (plane_out.at[1], plane_in.at[0], (row, col_up)),
        (plane_out.at[0], plane_in.at[1], (row, col_dn)),
    )):
        copy = pltpu.make_async_remote_copy(
            src, dst, edge_send.at[n], edge_recv.at[n], device_id=where, device_id_type=MESH
        )
        copy.start()
        halo_copies.append(copy)
    field_load.wait()
    smooth(range(QUAD, CZ - QUAD), inner)
    for n in (0, 1):
        halo_copies[n].wait_recv()
    for z in range(CZ):
        padded[1 + z, 7:8, :] = halo_lo[z : z + 1, :]
        padded[1 + z, 8 + CY : 9 + CY, :] = halo_hi[z : z + 1, :]

    def along_x(part):
        def block(n, carry):
            k = pl.multiple_of(n * 512, 512)
            out = dot(
                table[pl.ds(k, 512), :], forcing[part * QUAD * CY : (part + 1) * QUAD * CY, :], ((1,), (1,))
            )
            for pair in range(QUAD // 2):
                both = [
                    out[:, z * CY : (z + 1) * CY].reshape(64, OWN, CY)
                    for z in (2 * pair, 2 * pair + 1)
                ]
                outgoing[part, pl.ds(n * 64, 64), pair * 16 : pair * 16 + 16, :] = jnp.concatenate(
                    both, axis=1
                ).astype(BF16)
            return carry

        lax.fori_loop(0, NX // 512, block, 0)

    def landing(part):
        return incoming.at[
            part,
            pl.ds(pl.multiple_of(col * MSG, MSG), MSG),
            pl.ds(pl.multiple_of(row * CY, CY), CY),
        ]

    def send(part):
        def one(r, c):
            pltpu.make_async_remote_copy(
                outgoing.at[part, r * COLS + c], landing(part), send_sems.at[part], recv_sems.at[part],
                device_id=(r, c), device_id_type=MESH,
            ).start()

        for_partners(row, col, one)
        own = pltpu.make_async_copy(outgoing.at[part, me], landing(part), own_sems.at[part])
        own.start()
        return own

    owns = {}
    for part in ORDER:
        if part == ORDER[2]:
            for copy in halo_copies[2:]:
                copy.wait_recv()
            below, above = plane_in[0].astype(F32), plane_in[1].astype(F32)
            has_below, has_above = col > 0, col < COLS - 1
            padded[0, 8 : 8 + CY, :] = jnp.where(has_below, below, 0.0)
            padded[CZ + 1, 8 : 8 + CY, :] = jnp.where(has_above, above, 0.0)
            padded[0, 7:8, :] = jnp.where(has_below, corners[0, 7:8, :], 0.0)
            padded[0, 8 + CY : 9 + CY, :] = jnp.where(has_below, corners[1, 7:8, :], 0.0)
            padded[CZ + 1, 7:8, :] = jnp.where(has_above, corners[2, 0:1, :], 0.0)
            padded[CZ + 1, 8 + CY : 9 + CY, :] = jnp.where(has_above, corners[3, 0:1, :], 0.0)
            smooth((0, CZ - 1), inner)
            smooth((0, CZ - 1), outer)
            smooth(range(1, QUAD), inner)
            smooth(range(CZ - QUAD, CZ - 1), inner)
        levels = range(part * QUAD, (part + 1) * QUAD)
        smooth([z for z in levels if 0 < z < CZ - 1], outer)
        along_x(part)
        owns[part] = send(part)

    for part in ORDER:
        owns[part].wait()
        arrived = outgoing.at[part, pl.ds(0, DEVICES - 1)]
        pltpu.make_async_copy(arrived, arrived, recv_sems.at[part]).wait()

        def along_y(n, carry, part=part):
            rows = pl.ds(pl.multiple_of(n * 512, 512), 512)
            out = dot(incoming[part, rows, :], table[...], ((1,), (0,)))
            for tile in range(NY // LANES):
                lines[part, tile, rows, :] = out[:, tile * LANES : (tile + 1) * LANES]
            return carry

        lax.fori_loop(0, COLS * MSG // 512, along_y, 0)

    def solve(k, carry):
        wave = me * OWN + k
        folded = jnp.minimum(wave, NX - wave).astype(F32) * (2.0 * math.pi / NX)
        base = 1.0 + DIFFUSION * folded * folded

        every = pl.ds(k, COLS * QUAD, stride=OWN)
        for n in range(NY // 256):
            planes = jnp.concatenate(
                [
                    jnp.concatenate([lines[part, 2 * n + t, every, :] for t in range(2)], axis=1)
                    for part in range(PARTS)
                ],
                axis=0,
            ).astype(BF16)
            modal = dot(ordered[...], planes, ((1,), (0,)))
            denom = (base + DIFFUSION * wave_y[0:1, n * 256 : (n + 1) * 256]) + damping[:, 0:1]
            scaled = (modal / denom).astype(BF16)
            modes[:, n * 256 : (n + 1) * 256] = dot(synthesis[...], scaled, ((1,), (0,))).astype(BF16)
        solved[k] = dot(modes[...], table[...], ((1,), (0,))).astype(BF16)
        return carry

    def piece(begin, end, r, c):
        return solved.at[
            pl.ds(begin, end - begin),
            pl.ds(pl.multiple_of(c * CZ, CZ), CZ),
            pl.ds(pl.multiple_of(r * CY, CY), CY),
        ]

    back_owns = []
    spans = list(enumerate(zip(PHASES[:-1], PHASES[1:])))
    for phase, (begin, end) in spans:
        lax.fori_loop(begin, end, solve, 0)
        place = arrivals.at[pl.ds(begin, end - begin), me]

        def give(r, c, phase=phase, begin=begin, end=end, place=place):
            pltpu.make_async_remote_copy(
                piece(begin, end, r, c), place, back_send.at[phase], back_recv.at[phase],
                device_id=(r, c), device_id_type=MESH,
            ).start()

        for_partners(row, col, give)
        own = pltpu.make_async_copy(piece(begin, end, row, col), place, back_own.at[phase])
        own.start()
        back_owns.append(own)

    def turn(k):
        def widen(n, carry):
            rows = pl.ds(pl.multiple_of(n * 32 * CZ, 32 * CZ), 32 * CZ)
            wide[rows, :] = arrivals[k, pl.ds(n * 32, 32)].astype(F32).reshape(32 * CZ, CY)
            return carry

        lax.fori_loop(0, DEVICES // 32, widen, 0)
        for z in range(CZ):
            turned[k % 2, z] = wide[pl.ds(z, DEVICES, stride=CZ), :].T.astype(BF16)
        return pltpu.make_async_copy(
            turned.at[k % 2], home.at[:, :, pl.ds(k * DEVICES, DEVICES)], home_sems.at[k]
        )

    homes = []
    for phase, (begin, end) in spans:
        back_owns[phase].wait()
        arrived = arrivals.at[pl.ds(begin, end - begin), pl.ds(0, DEVICES - 1)]
        pltpu.make_async_copy(arrived, arrived, back_recv.at[phase]).wait()
        for k in range(begin, end):
            if k >= 2:
                homes[k - 2].wait()
            homes.append(turn(k))
            homes[k].start()
    for phase, (begin, end) in spans:
        sent = arrivals.at[pl.ds(begin, end - begin), pl.ds(0, DEVICES - 1)]
        pltpu.make_async_copy(sent, sent, back_send.at[phase]).wait()
    for copy in homes[-2:]:
        copy.wait()
    for part in range(PARTS):
        sent = outgoing.at[part, pl.ds(0, DEVICES - 1)]
        pltpu.make_async_copy(sent, sent, send_sems.at[part]).wait()
    for copy in halo_copies:
        copy.wait_send()


def spectral_step(deposit, thermal, table, analysis, synthesis, decay, wave_y):
    any_space, vmem = pl.BlockSpec(memory_space=pl.ANY), pl.BlockSpec(memory_space=pltpu.VMEM)
    return pl.pallas_call(
        spectral_kernel,
        out_shape=jax.ShapeDtypeStruct((CZ, CY, NX), BF16),
        in_specs=[any_space, any_space, vmem, vmem, vmem, vmem, vmem],
        out_specs=any_space,
        scratch_shapes=[
            pltpu.VMEM((NZ, NZ), BF16),
            pltpu.VMEM((NZ, LANES), F32),
            pltpu.VMEM((CZ + 2, CY + 16, NX), F32),
            pltpu.VMEM((CZ, CY, NX), F32),
            pltpu.VMEM((CZ * CY, NX), BF16),
            pltpu.VMEM((PARTS, DEVICES, MSG, CY), BF16),
            pltpu.VMEM((PARTS, COLS * MSG, NY), BF16),
            pltpu.VMEM((PARTS, NY // LANES, COLS * MSG, LANES), F32),
            pltpu.VMEM((OWN, NZ, NY), BF16),
            pltpu.VMEM((NZ, NY), BF16),
            pltpu.VMEM((OWN, DEVICES, CZ, CY), BF16),
            pltpu.VMEM((DEVICES * CZ, CY), F32),
            pltpu.VMEM((2, CZ, CY, DEVICES), BF16),
            pltpu.VMEM((CZ, NX), F32),
            pltpu.VMEM((CZ, NX), F32),
            pltpu.VMEM((CZ, NX), F32),
            pltpu.VMEM((CZ, NX), F32),
            pltpu.VMEM((4, 8, NX), F32),
            pltpu.VMEM((2, CY, NX), BF16),
            pltpu.VMEM((2, CY, NX), BF16),
            pltpu.SemaphoreType.DMA((2,)),
            pltpu.SemaphoreType.DMA((8,)),
            pltpu.SemaphoreType.DMA((8,)),
            pltpu.SemaphoreType.DMA((PARTS,)),
            pltpu.SemaphoreType.DMA((PARTS,)),
            pltpu.SemaphoreType.DMA((PARTS,)),
            pltpu.SemaphoreType.DMA((len(PHASES) - 1,)),
            pltpu.SemaphoreType.DMA((len(PHASES) - 1,)),
            pltpu.SemaphoreType.DMA((len(PHASES) - 1,)),
            pltpu.SemaphoreType.DMA((OWN,)),
        ],
        compiler_params=pltpu.CompilerParams(
            collective_id=0, has_side_effects=True, vmem_limit_bytes=60 * 2**20
        ),
        name="spectral_step",
    )(deposit, thermal, table, analysis, synthesis, decay, wave_y)


def home_kernel(home, table, out):
    for x in range(0, NX, 256):
        out[:, x : x + 256] = dot(home[...], table[:, x : x + 256], ((1,), (0,)))


def home_step(home, table):
    rows = QUAD * CY
    out = pl.pallas_call(
        home_kernel,
        grid=(CZ // QUAD,),
        out_shape=jax.ShapeDtypeStruct((CZ * CY, NX), F32),
        in_specs=[
            pl.BlockSpec((rows, NX), lambda i: (i, 0)),
            pl.BlockSpec((NX, NX), lambda i: (0, 0)),
        ],
        out_specs=pl.BlockSpec((rows, NX), lambda i: (i, 0)),
        compiler_params=pltpu.CompilerParams(vmem_limit_bytes=50 * 2**20),
        name="home_step",
    )(home.reshape(CZ * CY, NX), table)
    return out.reshape(CZ, CY, NX)


def deposit_kernel(first, last, keys, energy, out, key_rows, energy_rows):
    level, rows = pl.program_id(0), keys.shape[0]

    @pl.when(level == 0)
    def _():
        key_rows[0:rows, :] = keys[...]
        energy_rows[0:rows, :] = energy[...]
        key_rows[rows:, :] = jnp.full((WINDOW, LANES), GROUPS * CY * LANES, jnp.int32)
        energy_rows[rows:, :] = jnp.zeros((WINDOW, LANES), F32)

    lane = lax.broadcasted_iota(jnp.int32, (LANES, LANES), 0).astype(BF16)
    one, nil = jnp.ones((LANES, LANES), BF16), jnp.zeros((LANES, LANES), BF16)

    def tile(group, start):
        chosen, weights = [], []
        for n in range(WINDOW):
            key, heat = key_rows[pl.ds(start + n, 1), :], energy_rows[pl.ds(start + n, 1), :]
            hit = lane == (key & (LANES - 1)).astype(F32).astype(BF16)
            weights.append(jnp.where(hit, heat.astype(BF16), nil))
            line = (key >> 7) - group * CY
            line = jnp.where((line >= 0) & (line < CY), line, -1).astype(F32).astype(BF16)
            chosen.append(jnp.where(lane == line, one, nil))
        return dot(jnp.concatenate(chosen, axis=1), jnp.concatenate(weights, axis=1), ((1,), (1,)))

    per_level = NX // LANES
    starts = [first[level * per_level + n] for n in range(per_level)]
    for n, start in enumerate(starts):
        out[0, :, n * LANES : (n + 1) * LANES] = tile(level * per_level + n, start)
    for n, start in enumerate(starts):
        group = level * per_level + n

        def further(w, c, n=n, group=group, start=start):
            out[0, :, n * LANES : (n + 1) * LANES] += tile(group, start + w * WINDOW)
            return c

        lax.fori_loop(1, (last[group] - start + WINDOW - 1) // WINDOW, further, 0)


def deposit_step(location, energy, tally):
    slots = energy.shape[0]
    live = jnp.arange(slots, dtype=jnp.int32) < tally[0]
    x = location[0]
    key = ((location[2] * (NX // LANES) + x // LANES) * CY + location[1]) * LANES + x % LANES
    key = jnp.where(live, key, GROUPS * CY * LANES)
    key, energy = lax.sort((key, energy), num_keys=1, is_stable=False)
    key, energy = key.reshape(-1, LANES), energy.reshape(-1, LANES)
    group = jnp.arange(GROUPS, dtype=jnp.int32)[:, None] * (CY * LANES)
    first = jnp.sum((key[:, LANES - 1] < group).astype(jnp.int32), axis=1)
    last = jnp.sum((key[:, 0] < group + CY * LANES).astype(jnp.int32), axis=1)
    smem, vmem = pl.BlockSpec(memory_space=pltpu.SMEM), pl.BlockSpec(memory_space=pltpu.VMEM)
    return pl.pallas_call(
        deposit_kernel,
        out_shape=jax.ShapeDtypeStruct((CZ, CY, NX), F32),
        grid=(CZ,),
        in_specs=[smem, smem, vmem, vmem],
        out_specs=pl.BlockSpec((1, CY, NX), lambda z: (z, 0, 0)),
        scratch_shapes=[
            pltpu.VMEM((slots // LANES + WINDOW, LANES), jnp.int32),
            pltpu.VMEM((slots // LANES + WINDOW, LANES), F32),
        ],
        compiler_params=pltpu.CompilerParams(vmem_limit_bytes=50 * 2**20),
        name="deposit_step",
    )(first, last, key, energy)


def body(thermal, location, energy, tally, decay, analysis, synthesis):
    deposit = deposit_step(location, energy, tally)
    table = jnp.asarray(cas_table(NX))
    index = np.arange(NY)
    wave_y = ((np.minimum(index, NY - index) * (2.0 * math.pi / NY)) ** 2).astype(np.float32)
    home = spectral_step(
        deposit, thermal, table, analysis, synthesis, decay[None, :], jnp.asarray(wave_y)[None, :]
    )
    ordered = cas_table(NX).reshape(DEVICES, OWN, NX).transpose(1, 0, 2).reshape(NX, NX)
    return home_step(home, jnp.asarray(ordered))


def solution(mesh):
    in_specs = (
        P("col", "row", None),
        P(None, ("row", "col")),
        P(("row", "col")),
        P(("row", "col")),
        P(),
        P(),
        P(),
    )
    return jax.shard_map(
        body, mesh=mesh, in_specs=in_specs, out_specs=P("col", "row", None), check_vma=False
    )
```
